32 devices in a mesh: row: 4 (over x, core), col: 8 (over z, y).
Axes of the slice: x: 2, y: 2, z: 4, core: 2. Of those that a mesh axis runs over, the one named last changes fastest.
Arguments:
- panel: float32 [6, 2048, 2048], P(None, 'row', 'col'), may hold values from -0.0625 to 0.0625
- inverse_blocks: float32 [4, 2048, 2048], P(None, 'row', 'col'), may hold values from -1.5 to 1.5, as said below
- trailing_factor: float32 [12, 2048, 4, 2048], P(None, 'row', None, 'col'), may hold values from -0.0625 to 0.0625
- columns: float32 [4, 2048, 1024], P(None, 'row', 'col'), may hold values from -6 to 6
- trailing_columns: float32 [12, 2048, 1024], P(None, 'row', 'col'), may hold values from -6 to 6
Outputs:
- whitened: float32 [4, 2048, 1024], P(None, 'row', 'col')
- updated: float32 [12, 2048, 1024], P(None, 'row', 'col')
- variance_drop: float32 [1024], P('col')
The draws below stay inside these ranges and needn't reach their ends.
Inputs may be any that keep to these rules, and one draw needn't show every extreme that they name: `inverse_blocks`: each block is lower triangular; its diagonal entries lie between 0.5 and 1.5.
All inputs are finite; a program needn't handle non-finite values.
Results may differ from the reference program's by a relative error of at most 0.00011.
Values sent between devices are 32-bit elements; how exact they have to be, the bound alone decides.
A program may use at most 128 MiB of HBM per device.

```python
import jax
import jax.numpy as jnp
from jax import lax

NB = 2048
STEPS = 4
TRAIL = 12
M = 1024
PAIRS = 6


def draw_inverse_blocks(key, part):
    key = jax.random.fold_in(key, 7)
    key_off, key_diag = jax.random.split(key)
    shape = (STEPS, NB, NB)
    rows = lax.broadcasted_iota(jnp.int32, shape, 1)
    cols = lax.broadcasted_iota(jnp.int32, shape, 2)
    off = jnp.clip(jax.random.normal(key_off, shape, jnp.float32), -6.0, 6.0) * (0.5 * NB ** (-0.5))
    diag = jax.random.uniform(key_diag, shape, jnp.float32, 0.5, 1.5)
    return jnp.where(rows == cols, diag, jnp.where(rows > cols, off, 0.0)).astype(jnp.float32)


def block_scale(key, shape, cuts, least, high):
    loudness, own = 1.0, jax.random.fold_in(key, 6)
    for axis_at, blocks in cuts:
        heights = jnp.exp(jax.random.uniform(jax.random.fold_in(own, axis_at), (blocks,), jnp.float32, least / len(cuts), high / len(cuts)))
        loudness = loudness * jnp.repeat(heights, shape[axis_at] // blocks).reshape([-1 if axis == axis_at else 1 for axis in range(len(shape))])
    return loudness


def scatter_about(own_key, shape, deviation, reach, shards=(), dtype=jnp.bfloat16):
    drawn = deviation * jax.random.normal(own_key, shape, jnp.float32)
    if shards:
        drawn = drawn * block_scale(own_key, shape, shards, -0.22, 0.18)
    return jnp.clip(drawn, -reach, reach).astype(dtype)


def setup_inputs(seed: int = 0) -> dict:
    key_of = jax.random.split(jax.random.key(seed), 6)
    return {
        "panel": scatter_about(key_of[0], (PAIRS, NB, NB), (4 * NB) ** -0.5, 0.0625, ((1, 4), (2, 8)), jnp.float32),
        "inverse_blocks": draw_inverse_blocks(jax.random.fold_in(key_of[5], 71), 0),
        "trailing_factor": scatter_about(key_of[2], (TRAIL, NB, STEPS, NB), (4 * NB) ** -0.5, 0.0625, ((1, 4), (3, 8)), jnp.float32),
        "columns": scatter_about(key_of[3], (STEPS, NB, M), 1.0, 6.0, ((1, 4), (2, 8)), jnp.float32),
        "trailing_columns": scatter_about(key_of[4], (TRAIL, NB, M), 1.0, 6.0, ((1, 4), (2, 8)), jnp.float32),
    }


def product(left, right):
    return jnp.dot(left, right, precision=lax.Precision.HIGHEST, preferred_element_type=jnp.float32)


def reference(panel, inverse_blocks, trailing_factor, columns, trailing_columns):
    solved = []
    for j in range(STEPS):
        reduced = columns[j]
        if j > 0:
            total = jnp.zeros_like(reduced)
            for i in range(j):
                total = total + product(panel[j * (j - 1) // 2 + i], solved[i])
            reduced = reduced - total
        solved.append(product(inverse_blocks[j], reduced))
    whitened = jnp.stack(solved)

    def trail_row(pair):
        factor_row, column_row = pair
        acc = jnp.zeros_like(column_row)
        for j in range(STEPS):
            acc = acc + product(factor_row[:, j, :], whitened[j])
        return column_row - acc

    updated = lax.map(trail_row, (trailing_factor, trailing_columns))
    variance_drop = jnp.sum(whitened * whitened, axis=(0, 1)) / (STEPS * NB)
    return whitened, updated, variance_drop
```

```python
import functools

import jax
import jax.numpy as jnp
from jax import lax
from jax.experimental import pallas as pl
from jax.experimental.pallas import tpu as pltpu
from jax.sharding import PartitionSpec as P


def trailing_update(trailing_factor, trailing_columns, own, other, kept, got):
    cols = lax.axis_size("col")
    h = lax.rem(lax.axis_index("col"), 2)
    trail, rows, _, _ = trailing_factor.shape
    half = rows // 2
    width = trailing_columns.shape[2]
    groups = [[2 * g + p for g in range(cols // 2)] for p in range(2)]
    partial = contract(kept, own) + contract(got, other)
    summed = lax.psum_scatter(
        partial, "col", scatter_dimension=2, axis_index_groups=groups, tiled=True
    )
    mine = lax.dynamic_slice_in_dim(summed, h * width, width, 2)
    theirs = lax.dynamic_slice_in_dim(summed, (1 - h) * width, width, 2)
    back = lax.ppermute(theirs, "col", swaps(cols))
    low = jnp.where(h == 0, mine, back)
    high = jnp.where(h == 0, back, mine)
    return trailing_columns - jnp.concatenate([low, high], axis=1)


def contract(factor, solved):
    return jnp.einsum(
        "tajb,jbm->tam",
        factor,
        solved,
        precision=lax.Precision.HIGH,
        preferred_element_type=jnp.float32,
    )


def swaps(cols):
    return [(c, c ^ 1) for c in range(cols)]


def swap_factor(trailing_factor):
    cols = lax.axis_size("col")
    h = lax.rem(lax.axis_index("col"), 2)
    half = trailing_factor.shape[1] // 2
    kept = lax.dynamic_slice_in_dim(trailing_factor, h * half, half, 1)
    sent = lax.dynamic_slice_in_dim(trailing_factor, (1 - h) * half, half, 1)
    return kept, lax.ppermute(sent, "col", swaps(cols))


def split(value):
    high = value.astype(jnp.bfloat16)
    low = (value - high.astype(jnp.float32)).astype(jnp.bfloat16)
    return high, low


def dot3(left, right):
    left_high, left_low = split(left)
    right_high, right_low = split(right)

    def one(a, b):
        return jnp.dot(a, b, preferred_element_type=jnp.float32)

    return one(left_high, right_high) + (one(left_high, right_low) + one(left_low, right_high))


def chain_kernel(
    R, C, steps, panel, inverse, columns, solved_out, whitened_out,
    blocks, wants, held, parts, stage, acc, kept,
    own_sem, swap_send, swap_recv, want_send, want_recv, want_own, part_send, part_recv,
    root_send, fork_send, held_recv, piece_send, piece_recv, out_sem,
):
    pairs = panel.shape[0]
    G = C // 2
    Q = G
    rows = blocks.shape[2]
    lag = 2
    r = lax.axis_index("row")
    c = lax.axis_index("col")
    g = c // 2
    h = lax.rem(c, 2)
    is_root = r == g
    is_lead = lax.rem(r, 2) == lax.rem(g, 2)
    sibling = r + 1 - 2 * lax.rem(r, 2)

    def remote(src, dst, send, recv, row, col):
        return pltpu.make_async_remote_copy(
            src_ref=src, dst_ref=dst, send_sem=send, recv_sem=recv,
            device_id=(row, col), device_id_type=pl.DeviceIdType.MESH,
        )

    def mine(src, dst, sem):
        return pltpu.make_async_copy(src, dst, sem)

    barrier = pltpu.get_barrier_semaphore()
    for o in range(1, C):
        pl.semaphore_signal(
            barrier, inc=1, device_id=(r, lax.rem(c + o, C)), device_id_type=pl.DeviceIdType.MESH
        )
    for o in range(1, R):
        for p in range(2):
            pl.semaphore_signal(
                barrier, inc=1, device_id=(lax.rem(r + o, R), 2 * g + p),
                device_id_type=pl.DeviceIdType.MESH,
            )
    pl.semaphore_wait(barrier, C - 1 + 2 * (R - 1))

    def want_copy(p):
        return remote(
            columns.at[:, pl.ds(p * rows, rows), :], wants.at[c], want_send.at[p], want_recv.at[c],
            r, 2 * r + p,
        )

    def want_mine(p):
        return mine(columns.at[:, pl.ds(p * rows, rows), :], wants.at[c], want_own)

    for p in range(2):
        here = c == 2 * r + p

        @pl.when(jnp.logical_not(here))
        def _():
            want_copy(p).start()

        @pl.when(here)
        def _():
            want_mine(p).start()

    def block_of(s, i):
        j = s // 2
        return jnp.where(lax.rem(s, 2) == 1, pairs + j, j * (j - 1) // 2 + i)

    def count_of(s):
        return jnp.where(lax.rem(s, 2) == 1, 1, s // 2)

    def each_block(k, action):
        @pl.when(k < pairs)
        def _():
            action(panel, k)

        @pl.when(k >= pairs)
        def _():
            action(inverse, k - pairs)

    def start_blocks(s):
        def body(i, _):
            k = block_of(s, i)

            def action(source, at):
                mine(
                    source.at[at, pl.ds(pl.multiple_of(h * rows, rows), rows), :],
                    blocks.at[k, h], own_sem.at[k],
                ).start()
                remote(
                    source.at[at, pl.ds(pl.multiple_of((1 - h) * rows, rows), rows), :],
                    blocks.at[k, h], swap_send.at[k], swap_recv.at[k], r, 2 * g + 1 - h,
                ).start()

            each_block(k, action)
            return 0

        lax.fori_loop(0, count_of(s), body, 0)

    def swapped(k):
        return remote(
            blocks.at[k, h], blocks.at[k, 1 - h], swap_send.at[k], swap_recv.at[k], r, 2 * g + 1 - h
        )

    def wait_blocks(s):
        def body(i, _):
            k = block_of(s, i)
            mine(blocks.at[k, h], blocks.at[k, h], own_sem.at[k]).wait()
            swapped(k).wait_recv()
            return 0

        lax.fori_loop(0, count_of(s), body, 0)

    def chunk(s, half, q):
        return held.at[s, half, pl.ds(2 * q, 2)]

    def part_copy(s, q, up):
        step = 1 if up else -1
        return remote(
            stage.at[q], parts.at[1 if up else 0, s - 1, q], part_send.at[q],
            part_recv.at[1 if up else 0, s - 1, q], r, 2 * (g + step) + h,
        )

    def root_copy(s, q, o):
        return remote(
            chunk(s, h, q), chunk(s, h, q), root_send.at[q, o - 1], held_recv.at[s, h, q],
            lax.rem(r + 2 * o, R), c,
        )

    def fork_copy(s, q, n):
        half = h if n < 2 else 1 - h
        row, col = (r, 2 * g + 1 - h) if n == 0 else (sibling, c)
        return remote(
            chunk(s, half, q), chunk(s, half, q), fork_send.at[q, n], held_recv.at[s, half, q],
            row, col,
        )

    def piece_copy(s, q, p):
        return remote(
            held.at[s, h, 2 * q + p], kept.at[s // 2, h], piece_send.at[q, p],
            piece_recv.at[s // 2, h], r, 2 * q + p,
        )

    def pieces(s, q, action):
        for p in range(2):
            @pl.when(2 * q + p != c)
            def _():
                action(piece_copy(s, q, p))

    def finish_root(s, q):
        @pl.when(s >= 1)
        def _():
            for o in range(1, R // 2):
                root_copy(s, q, o).wait_send()

        for o in range(1, R // 2):
            root_copy(s, q, o).start()

        @pl.when(lax.rem(s, 2) == 1)
        def _():
            @pl.when(s >= 3)
            def _():
                pieces(s, q, lambda copy: copy.wait_send())

            pieces(s, q, lambda copy: copy.start())
            for p in range(2):
                @pl.when(2 * q + p == c)
                def _():
                    kept[s // 2, h] = held[s, h, 2 * q + p]

    def first(s, q):
        @pl.when(s == 0)
        def _():
            @pl.when(is_root)
            def _():
                for p in range(2):
                    m = 2 * q + p

                    @pl.when(m != c)
                    def _():
                        remote(
                            wants.at[m], wants.at[m], want_send.at[0], want_recv.at[m], r, m
                        ).wait_recv()

                    @pl.when(m == c)
                    def _():
                        mine(wants.at[m], wants.at[m], want_own).wait()

                    held[0, h, m] = wants[m, 0]
                finish_root(s, q)

        @pl.when(s >= 1)
        def _():
            @pl.when(q == 0)
            def _():
                wait_blocks(s)

                @pl.when(s + 2 < 2 * steps)
                def _():
                    start_blocks(s + 2)

            acc[...] = jnp.zeros_like(acc)

            def body(i, _):
                k = block_of(s, i)
                source = jnp.where(lax.rem(s, 2) == 1, s - 1, 2 * i + 1)
                for half in range(2):
                    left = blocks[k, half]
                    for p in range(2):
                        acc[p] += dot3(left, held[source, half, 2 * q + p])
                return 0

            lax.fori_loop(0, count_of(s), body, 0)

            @pl.when((g >= r) & (g < G - 1))
            def _():
                remote(
                    stage.at[q], parts.at[0, s - 1, q], part_send.at[q], part_recv.at[0, s - 1, q],
                    r, 2 * jnp.maximum(g - 1, 0) + h,
                ).wait_recv()
                acc[...] += parts[0, s - 1, q]

            @pl.when((g <= r) & (g > 0))
            def _():
                remote(
                    stage.at[q], parts.at[1, s - 1, q], part_send.at[q], part_recv.at[1, s - 1, q],
                    r, 2 * jnp.minimum(g + 1, G - 1) + h,
                ).wait_recv()
                acc[...] += parts[1, s - 1, q]

            for up in (False, True):
                @pl.when((g < r) if up else (g > r))
                def _():
                    @pl.when(s >= 2)
                    def _():
                        part_copy(s, q, up).wait_send()

                    stage[q] = acc[...]
                    part_copy(s, q, up).start()

            @pl.when(is_root)
            def _():
                @pl.when(lax.rem(s, 2) == 1)
                def _():
                    for p in range(2):
                        held[s, h, 2 * q + p] = acc[p]

                @pl.when(lax.rem(s, 2) == 0)
                def _():
                    for p in range(2):
                        held[s, h, 2 * q + p] = wants[2 * q + p, s // 2] - acc[p]

                finish_root(s, q)

    def arrived(s, half, q):
        remote(
            chunk(s, half, q), chunk(s, half, q), root_send.at[0, 0], held_recv.at[s, half, q],
            sibling, c,
        ).wait_recv()

    def second(s, q):
        @pl.when(jnp.logical_not(is_root))
        def _():
            arrived(s, h, q)

        @pl.when(is_lead)
        def _():
            @pl.when(s >= 1)
            def _():
                for n in range(3):
                    fork_copy(s, q, n).wait_send()

            fork_copy(s, q, 0).start()
            fork_copy(s, q, 1).start()

        arrived(s, 1 - h, q)

        @pl.when(is_lead)
        def _():
            fork_copy(s, q, 2).start()

    start_blocks(jnp.int32(1))
    start_blocks(jnp.int32(2))
    total = 2 * steps * Q

    def turn(t, _):
        @pl.when(t < total)
        def _():
            first(t // Q, lax.rem(t, Q))

        @pl.when(t >= lag)
        def _():
            second((t - lag) // Q, lax.rem(t - lag, Q))

        return 0

    lax.fori_loop(0, total + lag, turn, 0)

    for j in range(steps):
        mine(held.at[2 * j + 1], solved_out.at[j], out_sem.at[j]).start()

    last = jnp.int32(2 * steps - 1)

    def drain(q, _):
        @pl.when(is_root)
        def _():
            for o in range(1, R // 2):
                root_copy(last, q, o).wait_send()
            pieces(last, q, lambda copy: copy.wait_send())

        @pl.when(is_lead)
        def _():
            for n in range(3):
                fork_copy(last, q, n).wait_send()

        for up in (False, True):
            @pl.when((g < r) if up else (g > r))
            def _():
                part_copy(last, q, up).wait_send()

        return 0

    lax.fori_loop(0, Q, drain, 0)

    def drain_block(k, _):
        swapped(k).wait_send()
        return 0

    lax.fori_loop(0, pairs + steps, drain_block, 0)
    for p in range(2):
        @pl.when(c != 2 * r + p)
        def _():
            want_copy(p).wait_send()

            for j in range(steps):
                remote(
                    kept.at[j, p], kept.at[j, p], piece_send.at[0, 0], piece_recv.at[j, p],
                    r, 2 * r + p,
                ).wait_recv()

    done = mine(kept, whitened_out, out_sem.at[steps])
    done.start()
    for j in range(steps):
        mine(held.at[2 * j + 1], solved_out.at[j], out_sem.at[j]).wait()
    done.wait()


def solve_chain(panel, inverse_blocks, columns):
    R = lax.axis_size("row")
    C = lax.axis_size("col")
    G = C // 2
    Q = G
    pairs = panel.shape[0]
    steps, height, width = columns.shape
    rows = height // 2
    depth = panel.shape[2]
    dma = pltpu.SemaphoreType.DMA
    f32 = jnp.float32
    flops = 6 * 2 * rows * (2 * depth) * C * width * (pairs + steps)
    solved, whitened = pl.pallas_call(
        functools.partial(chain_kernel, R, C, steps),
        out_shape=(
            jax.ShapeDtypeStruct((steps, 2, C, rows, width), f32),
            jax.ShapeDtypeStruct((steps, 2, rows, width), f32),
        ),
        in_specs=[pl.BlockSpec(memory_space=pl.ANY)] * 3,
        out_specs=(pl.BlockSpec(memory_space=pl.ANY), pl.BlockSpec(memory_space=pl.ANY)),
        scratch_shapes=[
            pltpu.VMEM((pairs + steps, 2, rows, depth), f32),
            pltpu.VMEM((C, steps, rows, width), f32),
            pltpu.VMEM((2 * steps, 2, C, rows, width), f32),
            pltpu.VMEM((2, 2 * steps - 1, Q, 2, rows, width), f32),
            pltpu.VMEM((Q, 2, rows, width), f32),
            pltpu.VMEM((2, rows, width), f32),
            pltpu.VMEM((steps, 2, rows, width), f32),
            dma((pairs + steps,)),
            dma((pairs + steps,)),
            dma((pairs + steps,)),
            dma((2,)),
            dma((C,)),
            dma,
            dma((Q,)),
            dma((2, 2 * steps - 1, Q)),
            dma((Q, max(R // 2 - 1, 1))),
            dma((Q, 3)),
            dma((2 * steps, 2, Q)),
            dma((Q, 2)),
            dma((steps, 2)),
            dma((steps + 1,)),
        ],
        compiler_params=pltpu.CompilerParams(
            collective_id=0, has_side_effects=True, vmem_limit_bytes=56 * 1024 * 1024
        ),
        cost_estimate=pl.CostEstimate(
            flops=flops * 10, bytes_accessed=400 * 1024 * 1024, transcendentals=0
        ),
    )(panel, inverse_blocks, columns)
    return solved, whitened.reshape(steps, height, width)


def shards(panel, inverse_blocks, trailing_factor, columns, trailing_columns):
    steps, height, _ = columns.shape
    order = height * lax.axis_size("row")
    kept, got = swap_factor(trailing_factor)
    solved, whitened = solve_chain(panel, inverse_blocks, columns)
    h = lax.rem(lax.axis_index("col"), 2)
    rows = solved.shape[3]

    def half(p):
        part = lax.dynamic_index_in_dim(solved, p, 1, keepdims=False)
        return jnp.transpose(part, (0, 2, 1, 3)).reshape(steps, rows, -1)

    updated = trailing_update(
        trailing_factor, trailing_columns, half(h), half(1 - h), kept, got
    )
    local_squares = jnp.sum(whitened * whitened, axis=(0, 1))
    variance_drop = lax.psum(local_squares, "row") / (steps * order)
    return (whitened, updated, variance_drop)


def solution(mesh):
    return jax.shard_map(
        shards,
        mesh=mesh,
        in_specs=(
            P(None, "row", "col"),
            P(None, "row", "col"),
            P(None, "row", None, "col"),
            P(None, "row", "col"),
            P(None, "row", "col"),
        ),
        out_specs=(P(None, "row", "col"), P(None, "row", "col"), P("col")),
        check_vma=False,
    )
```
